512 devices in a mesh: wide: 16 (over x, z_hi), long: 32 (over z_lo, y, core).
Axes of the slice: x: 4, y: 4, z: 16 (z_hi: 4, z_lo: 4; z = z_hi * 4 + z_lo), core: 2. Of those that a mesh axis runs over, the one named last changes fastest.
Arguments:
- velocity: bfloat16 [3, 128, 1024, 512], P(None, 'wide', 'long'), may hold values from -6 to 6
- vorticity: bfloat16 [3, 128, 1024, 512], P(None, 'wide', 'long'), may hold values from -6 to 6
- m_of_slot: int32 [512], replicated, may hold values from 0 to 511, as said below
- legendre: bfloat16 [512, 512, 512], P('long', 'wide'), as said below
- known_term: bfloat16 [512, 2, 3, 512, 128], P('long', None, None, 'wide'), may hold values from -6 to 6
- inverse: bfloat16 [512, 128, 128], P('wide'), may hold values from -0.5 to 0.5
Outputs:
- section_state: bfloat16 [512, 2, 3, 512, 128], P('long', None, None, 'wide')
The draws below stay inside these ranges and needn't reach their ends.
Inputs may be any that keep to these rules, and one draw needn't show every extreme that they name: m_of_slot is a permutation of 0 to 511; the m of slot s differs from s by less than 32. legendre[s, l, t] is zero wherever the degree l is below m_of_slot[s].
All inputs are finite; a program needn't handle non-finite values.
Results may differ from the reference program's by a relative error of at most 0.0059.
Values may be sent and summed in bfloat16 or wider, within the bound.
No kernel may reach another device: no remote copies, remote signals or barrier semaphores. Data moves between devices by JAX's collectives and lax.ppermute only.
A program may use at most 192 MiB of HBM per device.

```python
import math
import jax
import jax.numpy as jnp
from jax import lax

L = 512
NTH = 512
NR = 128
NPHI = 1024
SLOT_DEV = 16


def shuffled_modes(key):
    mode_index = jnp.arange(L, dtype=jnp.int32)
    jitter = jax.random.randint(key, (L,), 0, 2 * SLOT_DEV, dtype=jnp.int32)
    ranking = (mode_index + jitter) * L + mode_index
    return jnp.argsort(ranking, stable=True).astype(jnp.int32)


def draw_m_of_slot(key, part):
    return shuffled_modes(key)


def draw_legendre(key, part):
    mode_index = shuffled_modes(key)
    key = jax.random.fold_in(key, 11)
    values = jax.random.normal(key, (L, L, NTH), jnp.float32)
    degree = jnp.arange(L, dtype=jnp.int32)
    live = (degree[None, :] >= mode_index[:, None]).astype(jnp.float32)
    return (values * live[:, :, None] * NTH ** (-0.5)).astype(jnp.bfloat16)


def steps_of(rng, dims, split, smallest, top_value):
    gain, own = 1.0, jax.random.fold_in(rng, 6)
    for dim, blocks in split:
        heights = jnp.exp(jax.random.uniform(jax.random.fold_in(own, dim), (blocks,), jnp.float32, smallest / len(split), top_value / len(split)))
        gain = gain * jnp.repeat(heights, dims[dim] // blocks).reshape([-1 if axis == dim else 1 for axis in range(len(dims))])
    return gain


def scatter_about(own_key, extent, scale, most, cuts=(), kind=jnp.bfloat16):
    array = scale * jax.random.normal(own_key, extent, jnp.float32)
    if cuts:
        array = array * steps_of(own_key, extent, cuts, -0.22, 0.18)
    return jnp.clip(array, -most, most).astype(kind)


def setup_inputs(seed: int = 0) -> dict:
    key_of = jax.random.split(jax.random.key(seed), 7)
    return {
        "velocity": scatter_about(key_of[0], (3, NR, NPHI, NTH), 1.0, 6.0, ((1, 16), (2, 32))),
        "vorticity": scatter_about(key_of[1], (3, NR, NPHI, NTH), 1.0, 6.0, ((1, 16), (2, 32))),
        "m_of_slot": draw_m_of_slot(jax.random.fold_in(key_of[6], 71), 0),
        "legendre": draw_legendre(jax.random.fold_in(key_of[6], 71), 0),
        "known_term": scatter_about(key_of[4], (L, 2, 3, L, NR), 1.0, 6.0, ((0, 32), (3, 16))),
        "inverse": scatter_about(key_of[5], (L, NR, NR), NR ** -0.5, 0.5, ((0, 16),)),
    }


section_step = 0.75

def lamb_product(velocity, vorticity):
    vel = velocity.astype(jnp.float32)
    vort = vorticity.astype(jnp.float32)
    first = vel[1] * vort[2] - vel[2] * vort[1]
    second = vel[2] * vort[0] - vel[0] * vort[2]
    third = vel[0] * vort[1] - vel[1] * vort[0]
    return jnp.stack([first, second, third], axis=0).astype(jnp.bfloat16)

def phase_table(m_of_slot, points):
    column = jnp.arange(points, dtype=jnp.int32)
    paired_modes = jnp.repeat(m_of_slot.astype(jnp.int32), 2)
    parity = jnp.arange(paired_modes.shape[0], dtype=jnp.int32) % 2
    product = column[:, None] * paired_modes[None, :] % points
    phase_angle = 2.0 * math.pi / points * product.astype(jnp.float32)
    norm_factor = math.sqrt(2.0 / points)
    values = jnp.where(parity[None, :] == 0, norm_factor * jnp.cos(phase_angle), -norm_factor * jnp.sin(phase_angle))
    return values.astype(jnp.bfloat16)

def reference(velocity, vorticity, m_of_slot, legendre, known_term, inverse):
    lamb_vector = lax.optimization_barrier(lamb_product(velocity, vorticity))
    table_wide = lax.optimization_barrier(phase_table(m_of_slot, NPHI)).astype(jnp.float32)

    def one_field(field):
        summed = jnp.einsum('rjt,jc->rtc', field.astype(jnp.float32), table_wide)
        return summed.astype(jnp.bfloat16)
    fourier = lax.optimization_barrier(lax.map(one_field, lamb_vector))
    per_slot = fourier.reshape(3, NR, NTH, L, 2).transpose(3, 4, 0, 1, 2)

    def one_slot(pair):
        piece_block, slot_table = pair
        summed = jnp.einsum('cfrt,lt->cflr', piece_block.astype(jnp.float32), slot_table.astype(jnp.float32))
        return summed.astype(jnp.bfloat16)
    coeffs = lax.optimization_barrier(lax.map(one_slot, (per_slot, legendre)))
    right_side = (known_term.astype(jnp.float32) + section_step * coeffs.astype(jnp.float32)).astype(jnp.bfloat16)
    right_side = lax.optimization_barrier(right_side)
    inverse_wide = inverse.astype(jnp.float32)

    def one_solve(slot_side):
        solved = jnp.einsum('cflr,lqr->cflq', slot_side.astype(jnp.float32), inverse_wide)
        return solved.astype(jnp.bfloat16)
    return lax.map(one_solve, right_side)
```

```python
import math

import jax
import jax.numpy as jnp
from jax import lax
from jax.experimental import pallas as pl
from jax.experimental.pallas import tpu as pltpu
from jax.sharding import PartitionSpec as P

section_step = 0.75
VMEM_LIMIT = 48 * 1024 * 1024
LANES = 128


def params():
    return pltpu.CompilerParams(vmem_limit_bytes=VMEM_LIMIT)


def lamb_kernel(vel_ref, vort_ref, out_ref):
    vel = [vel_ref[i, 0].astype(jnp.float32) for i in range(3)]
    vort = [vort_ref[i, 0].astype(jnp.float32) for i in range(3)]
    for f in range(3):
        a, b = (f + 1) % 3, (f + 2) % 3
        lamb = (vel[a] * vort[b] - vel[b] * vort[a]).astype(jnp.bfloat16)
        for tb in range(lamb.shape[1] // LANES):
            out_ref[tb, f] = lamb[:, tb * LANES : (tb + 1) * LANES]


def lamb_blocks(velocity, vorticity):
    _, nr, nj, nt = velocity.shape
    tbs = nt // LANES
    spec = pl.BlockSpec((3, 1, nj, nt), lambda r: (0, r, 0, 0))
    return pl.pallas_call(
        lamb_kernel,
        grid=(nr,),
        in_specs=[spec, spec],
        out_specs=pl.BlockSpec((tbs, 3, nj, LANES), lambda r: (r, 0, 0, 0)),
        out_shape=jax.ShapeDtypeStruct((nr * tbs, 3, nj, LANES), jnp.bfloat16),
        compiler_params=params(),
    )(velocity, vorticity)


def phase_rows(m_of_slot, points, subs):
    modes = m_of_slot.reshape(-1, subs).T.reshape(-1)
    paired = jnp.repeat(modes, 2)
    parity = jnp.arange(paired.shape[0], dtype=jnp.int32) % 2
    column = jnp.arange(points, dtype=jnp.int32)
    product = (paired[:, None] * column[None, :] + parity[:, None] * (points // 4)) % points
    angle = 2.0 * math.pi / points * product.astype(jnp.float32)
    return (math.sqrt(2.0 / points) * jnp.cos(angle)).astype(jnp.bfloat16)


def dft_kernel(x_ref, table_ref, out_ref):
    points = table_ref.shape[1]
    grid = jnp.concatenate([x_ref[:, f].reshape(points, LANES) for f in range(3)], axis=1)
    out_ref[...] = jnp.dot(table_ref[...], grid, preferred_element_type=jnp.float32).astype(jnp.bfloat16)


def dft(x, table):
    rows, points = table.shape
    step = 256
    return pl.pallas_call(
        dft_kernel,
        grid=(rows // step,),
        in_specs=[
            pl.BlockSpec(x.shape, lambda i: (0, 0, 0, 0)),
            pl.BlockSpec((step, points), lambda i: (i, 0)),
        ],
        out_specs=pl.BlockSpec((step, 3 * LANES), lambda i: (i, 0)),
        out_shape=jax.ShapeDtypeStruct((rows, 3 * LANES), jnp.bfloat16),
        compiler_params=params(),
    )(x, table)


def reorder(source_of, n):
    row = lax.broadcasted_iota(jnp.int32, (n, n), 0)
    column = lax.broadcasted_iota(jnp.int32, (n, n), 1)
    return (source_of(row) == column).astype(jnp.float32).astype(jnp.bfloat16)


def legendre_kernel(y_ref, leg_ref, out_ref, side):
    blocks = y_ref.shape[0] // 256
    nodes = side.shape[1]
    tbs = nodes // LANES
    per = 256 // (2 * tbs)

    def source(i):
        tb, rest = i // (2 * per), i % (2 * per)
        c, wr = rest // per, rest % per
        return (wr * tbs + tb) * 2 + c

    move = reorder(source, 256)
    half = side.shape[0] // 2
    for k in range(blocks):
        moved = jnp.dot(
            move, y_ref[k * 256 : (k + 1) * 256, :], preferred_element_type=jnp.float32
        ).astype(jnp.bfloat16)
        for tb in range(tbs):
            for c in range(2):
                start = (tb * 2 + c) * per
                side[c * half + k * per : c * half + (k + 1) * per, tb * LANES : (tb + 1) * LANES] = (
                    moved[start : start + per, :]
                )
    coeffs = lax.dot_general(
        leg_ref[...], side[...], (((1,), (1,)), ((), ())), preferred_element_type=jnp.float32
    ).astype(jnp.bfloat16)
    wides, degrees = out_ref.shape[0], out_ref.shape[3]
    for c in range(2):
        out_ref[:, c, 0] = coeffs[:, c * half : (c + 1) * half].reshape(wides, degrees, half)


def legendre_step(y, leg, wides):
    rows = y.shape[0]
    degrees, nodes = leg.shape
    tbs = nodes // LANES
    nr = rows // (2 * tbs)
    return pl.pallas_call(
        legendre_kernel,
        grid=(3,),
        in_specs=[
            pl.BlockSpec((rows, LANES), lambda f: (0, f)),
            pl.BlockSpec(leg.shape, lambda f: (0, 0)),
        ],
        out_specs=pl.BlockSpec((wides, 2, 1, degrees // wides, nr), lambda f: (0, 0, f, 0, 0)),
        out_shape=jax.ShapeDtypeStruct((wides, 2, 3, degrees // wides, nr), jnp.bfloat16),
        scratch_shapes=[pltpu.VMEM((2 * nr, nodes), jnp.bfloat16)],
        compiler_params=params(),
    )(y, leg)


def solve_kernel(coeffs_ref, known_ref, inverse_ref, out_ref, side, solved):
    lines, degrees, nr = coeffs_ref.shape
    swap = reorder(lambda i: (i % 16) * 16 + i // 16, 256)
    for a in range(lines // 16):
        for h in range(degrees // 16):
            here = (slice(a * 16, (a + 1) * 16), slice(h * 16, (h + 1) * 16))
            right = (
                known_ref[here].astype(jnp.float32) + section_step * coeffs_ref[here].astype(jnp.float32)
            ).astype(jnp.bfloat16)
            moved = jnp.dot(swap, right.reshape(256, nr), preferred_element_type=jnp.float32)
            side[here[1], here[0]] = moved.astype(jnp.bfloat16).reshape(16, 16, nr)
    for k in range(degrees):
        solved[k] = lax.dot_general(
            side[k], inverse_ref[k], (((1,), (1,)), ((), ())), preferred_element_type=jnp.float32
        ).astype(jnp.bfloat16)
    for a in range(lines // 16):
        for h in range(degrees // 16):
            here = (slice(a * 16, (a + 1) * 16), slice(h * 16, (h + 1) * 16))
            moved = jnp.dot(
                swap, solved[here[1], here[0]].reshape(256, nr), preferred_element_type=jnp.float32
            )
            out_ref[here] = moved.astype(jnp.bfloat16).reshape(16, 16, nr)


def radial_solve(coeffs, known, inverse):
    lines, degrees, nr = coeffs.shape
    return pl.pallas_call(
        solve_kernel,
        out_shape=jax.ShapeDtypeStruct(coeffs.shape, jnp.bfloat16),
        scratch_shapes=[pltpu.VMEM((degrees, lines, nr), jnp.bfloat16)] * 2,
        compiler_params=params(),
    )(coeffs, known, inverse)


def body(velocity, vorticity, m_of_slot, legendre, known_term, inverse):
    slots, degrees, nodes = legendre.shape
    wides = slots
    leg = lax.all_to_all(legendre, "wide", split_axis=0, concat_axis=0, tiled=True)
    leg = leg.reshape(wides * degrees, nodes)
    blocks = lamb_blocks(velocity, vorticity)
    blocks = lax.all_to_all(blocks, "long", split_axis=0, concat_axis=0, tiled=True)
    blocks, leg = lax.optimization_barrier((blocks, leg))
    points = blocks.shape[0] * blocks.shape[2]
    table = phase_rows(m_of_slot, points, slots)
    fourier = dft(blocks, table)
    fourier = fourier.reshape(-1, 2, 3 * LANES)
    fourier = lax.all_to_all(fourier, ("wide", "long"), split_axis=0, concat_axis=0, tiled=True)
    coeffs = legendre_step(fourier.reshape(-1, 3 * LANES), leg, wides)
    coeffs = lax.all_to_all(coeffs, "wide", split_axis=0, concat_axis=0, tiled=True)
    lines = slots * 6
    solved = radial_solve(
        coeffs.reshape(lines, degrees, -1), known_term.reshape(lines, degrees, -1), inverse
    )
    return solved.reshape(known_term.shape)


def solution(mesh):
    return jax.shard_map(
        body,
        mesh=mesh,
        in_specs=(
            P(None, "wide", "long", None),
            P(None, "wide", "long", None),
            P(),
            P("long", "wide", None),
            P("long", None, None, "wide", None),
            P("wide", None, None),
        ),
        out_specs=P("long", None, None, "wide", None),
        check_vma=False,
    )
```

```python
import math

import jax
import jax.numpy as jnp
from jax import lax
from jax.experimental import pallas as pl
from jax.experimental.pallas import tpu as pltpu
from jax.sharding import Mesh
from jax.sharding import PartitionSpec as P

section_step = 0.75
VMEM_LIMIT = 48 * 1024 * 1024
LANES = 128


def params():
    return pltpu.CompilerParams(vmem_limit_bytes=VMEM_LIMIT)


def lamb_kernel(vel_ref, vort_ref, out_ref):
    vel = [vel_ref[i, 0].astype(jnp.float32) for i in range(3)]
    vort = [vort_ref[i, 0].astype(jnp.float32) for i in range(3)]
    for f in range(3):
        a, b = (f + 1) % 3, (f + 2) % 3
        lamb = (vel[a] * vort[b] - vel[b] * vort[a]).astype(jnp.bfloat16)
        for tb in range(lamb.shape[1] // LANES):
            out_ref[tb, f] = lamb[:, tb * LANES : (tb + 1) * LANES]


def lamb_blocks(velocity, vorticity):
    _, nr, nj, nt = velocity.shape
    tbs = nt // LANES
    spec = pl.BlockSpec((3, 1, nj, nt), lambda r: (0, r, 0, 0))
    return pl.pallas_call(
        lamb_kernel,
        grid=(nr,),
        in_specs=[spec, spec],
        out_specs=pl.BlockSpec((tbs, 3, nj, LANES), lambda r: (r, 0, 0, 0)),
        out_shape=jax.ShapeDtypeStruct((nr * tbs, 3, nj, LANES), jnp.bfloat16),
        compiler_params=params(),
    )(velocity, vorticity)


def phase_rows(m_of_slot, points, groups, subs):
    modes = m_of_slot.reshape(-1, groups, subs).transpose(1, 0, 2).reshape(-1)
    paired = jnp.repeat(modes, 2)
    parity = jnp.arange(paired.shape[0], dtype=jnp.int32) % 2
    column = jnp.arange(points, dtype=jnp.int32)
    product = (paired[:, None] * column[None, :] + parity[:, None] * (points // 4)) % points
    angle = 2.0 * math.pi / points * product.astype(jnp.float32)
    return (math.sqrt(2.0 / points) * jnp.cos(angle)).astype(jnp.bfloat16)


def dft_kernel(x_ref, table_ref, out_ref):
    points = table_ref.shape[1]
    grid = jnp.concatenate([x_ref[:, f].reshape(points, LANES) for f in range(3)], axis=1)
    out_ref[...] = jnp.dot(table_ref[...], grid, preferred_element_type=jnp.float32).astype(jnp.bfloat16)


def dft(x, table):
    rows, points = table.shape
    step = 256
    return pl.pallas_call(
        dft_kernel,
        grid=(rows // step,),
        in_specs=[
            pl.BlockSpec(x.shape, lambda i: (0, 0, 0, 0)),
            pl.BlockSpec((step, points), lambda i: (i, 0)),
        ],
        out_specs=pl.BlockSpec((step, 3 * LANES), lambda i: (i, 0)),
        out_shape=jax.ShapeDtypeStruct((rows, 3 * LANES), jnp.bfloat16),
        compiler_params=params(),
    )(x, table)


def matches(source_of, shape):
    row = lax.broadcasted_iota(jnp.int32, shape, 0)
    column = lax.broadcasted_iota(jnp.int32, shape, 1)
    return (source_of(row) == column).astype(jnp.float32).astype(jnp.bfloat16)


def moved_rows(matrix, array):
    return jnp.dot(matrix, array, preferred_element_type=jnp.float32).astype(jnp.bfloat16)


def legendre_kernel(zh_ref, y_ref, leg_ref, out_ref, side):
    zh = zh_ref[0]
    pair = pl.program_id(0)
    for kk in range(2):
        k = pair * 2 + kk

        def source(i):
            tb, c, z, r = i // 32, (i // 16) % 2, (i // 8) % 2, i % 8
            return ((z * 8 + r) * 4 + tb) * 8 + k * 2 + c

        move = matches(source, (128, 512))
        for h in range(2):
            moved = moved_rows(move, y_ref[h * 512 : (h + 1) * 512, :])
            for tb in range(4):
                for c in range(2):
                    for f in range(3):
                        start = (c * 3 + f) * 32 + h * 16
                        side[kk, start : start + 16, tb * LANES : (tb + 1) * LANES] = moved[
                            (tb * 2 + c) * 16 : (tb * 2 + c) * 16 + 16, f * LANES : (f + 1) * LANES
                        ]
    for x in range(4):
        coeffs = [
            lax.dot_general(
                leg_ref[x, kk].reshape(128, -1),
                side[kk],
                (((1,), (1,)), ((), ())),
                preferred_element_type=jnp.float32,
            ).astype(jnp.bfloat16)
            for kk in range(2)
        ]
        both = jnp.concatenate(coeffs, axis=1)
        for d in range(4):
            out_ref[x * 4 + ((zh - d) & 3), 0] = both[d * 32 : (d + 1) * 32, :]


def legendre_step(zh, y, leg):
    nodes = leg.shape[-1]
    return pl.pallas_call(
        legendre_kernel,
        grid=(2,),
        in_specs=[
            pl.BlockSpec(memory_space=pltpu.SMEM),
            pl.BlockSpec(y.shape, lambda p: (0, 0)),
            pl.BlockSpec((4, 2, 4, 32, nodes), lambda p: (0, p, 0, 0, 0)),
        ],
        out_specs=pl.BlockSpec((16, 1, 32, 384), lambda p: (0, p, 0, 0)),
        out_shape=jax.ShapeDtypeStruct((16, 2, 32, 384), jnp.bfloat16),
        scratch_shapes=[pltpu.VMEM((2, 192, nodes), jnp.bfloat16)],
        compiler_params=params(),
    )(zh, y, leg)


def solve_kernel(coeffs_ref, known_ref, inverse_ref, out_ref, side, solved):
    nr = known_ref.shape[-1]
    lanes = matches(lambda i: ((i // 32) % 4) * 128 + (i // 128) * 32 + i % 32, (512, 512))
    swap = matches(lambda i: (i % 16) * 16 + i // 16, (256, 256))
    grouped = []
    for g in range(3):
        wide = jnp.concatenate(
            [coeffs_ref[x, :, :, g * LANES : (g + 1) * LANES].reshape(256, LANES) for x in range(4)], axis=1
        )
        grouped.append(jnp.dot(wide, lanes, preferred_element_type=jnp.float32).astype(jnp.bfloat16))
    for cf in range(6):
        rights = []
        for kk in range(2):
            q = kk * 6 + cf
            coeffs = grouped[q // 4][:, (q % 4) * nr : (q % 4 + 1) * nr].astype(jnp.float32)
            known = known_ref[:, kk, cf].reshape(256, nr).astype(jnp.float32)
            rights.append((known + section_step * coeffs).astype(jnp.bfloat16).reshape(8, 32, nr))
        for h in range(2):
            both = jnp.concatenate([right[:, h * 16 : (h + 1) * 16] for right in rights], axis=0)
            side[h * 16 : (h + 1) * 16, cf * 16 : (cf + 1) * 16] = moved_rows(
                swap, both.reshape(256, nr)
            ).reshape(16, 16, nr)
    for k in range(32):
        solved[k] = lax.dot_general(
            side[k], inverse_ref[k], (((1,), (1,)), ((), ())), preferred_element_type=jnp.float32
        ).astype(jnp.bfloat16)
    for cf in range(6):
        for h in range(2):
            here = solved[h * 16 : (h + 1) * 16, cf * 16 : (cf + 1) * 16]
            back = moved_rows(swap, here.reshape(256, nr)).reshape(2, 8, 16, nr)
            for kk in range(2):
                out_ref[:, kk, cf, h * 16 : (h + 1) * 16] = back[kk]


def radial_solve(coeffs, known, inverse):
    nr = known.shape[-1]
    return pl.pallas_call(
        solve_kernel,
        out_shape=jax.ShapeDtypeStruct(known.shape, jnp.bfloat16),
        scratch_shapes=[pltpu.VMEM((32, 96, nr), jnp.bfloat16)] * 2,
        compiler_params=params(),
    )(coeffs, known, inverse)


def legendre_by_slot(legendre, zh):
    pieces = []
    for d in range(4):
        piece = lax.dynamic_slice_in_dim(legendre, ((zh + d) & 3) * 4, 4, axis=0)
        if d:
            piece = lax.ppermute(piece, "zh", [(i, (i + d) % 4) for i in range(4)])
        pieces.append(piece)
    return pieces


def body(velocity, vorticity, m_of_slot, legendre, known_term, inverse):
    zh = lax.axis_index("zh")
    table = phase_rows(m_of_slot, velocity.shape[2] * 32, 4, 4)
    pieces = legendre_by_slot(legendre, zh)
    table, *pieces = lax.optimization_barrier((table, *pieces))
    leg = jnp.stack(pieces, axis=1)
    blocks = lamb_blocks(velocity, vorticity)
    blocks = lax.all_to_all(blocks, "long", split_axis=0, concat_axis=0, tiled=True)
    blocks, leg = lax.optimization_barrier((blocks, leg))
    leg = lax.all_gather(leg, "x", axis=0, tiled=False)
    fourier = dft(blocks, table)
    fourier = fourier.reshape(-1, 8, 3 * LANES)
    fourier = lax.all_to_all(fourier, ("zh", "long"), split_axis=0, concat_axis=0, tiled=True)
    coeffs = legendre_step(zh.reshape(1), fourier.reshape(-1, 3 * LANES), leg)
    coeffs = lax.all_to_all(coeffs, ("x", "zh"), split_axis=0, concat_axis=0, tiled=True)
    nr = known_term.shape[-1]
    solved = radial_solve(
        coeffs.reshape(4, 8, 32, 384), known_term.reshape(8, 2, 6, 32, nr), inverse
    )
    return solved.reshape(known_term.shape)


def solution(mesh):
    mesh = Mesh(mesh.devices.reshape(4, 4, 32), ("x", "zh", "long"))
    wide = ("x", "zh")
    return jax.shard_map(
        body,
        mesh=mesh,
        in_specs=(
            P(None, wide, "long", None),
            P(None, wide, "long", None),
            P(),
            P("long", wide, None),
            P("long", None, None, wide, None),
            P(wide, None, None),
        ),
        out_specs=P("long", None, None, wide, None),
        check_vma=False,
    )
```

```python
import math

import jax
import jax.numpy as jnp
from jax import lax
from jax.experimental import pallas as pl
from jax.experimental.pallas import tpu as pltpu
from jax.sharding import Mesh
from jax.sharding import PartitionSpec as P

section_step = 0.75
VMEM_LIMIT = 48 * 1024 * 1024
LANES = 128


def params(limit=VMEM_LIMIT):
    return pltpu.CompilerParams(vmem_limit_bytes=limit)


def lamb_kernel(vel_ref, vort_ref, out_ref):
    vel = [vel_ref[i, 0].astype(jnp.float32) for i in range(3)]
    vort = [vort_ref[i, 0].astype(jnp.float32) for i in range(3)]
    for f in range(3):
        a, b = (f + 1) % 3, (f + 2) % 3
        lamb = (vel[a] * vort[b] - vel[b] * vort[a]).astype(jnp.bfloat16)
        for tb in range(lamb.shape[1] // LANES):
            out_ref[tb, f] = lamb[:, tb * LANES : (tb + 1) * LANES]


def lamb_blocks(velocity, vorticity):
    _, nr, nj, nt = velocity.shape
    tbs = nt // LANES
    spec = pl.BlockSpec((3, 1, nj, nt), lambda r: (0, r, 0, 0))
    return pl.pallas_call(
        lamb_kernel,
        grid=(nr,),
        in_specs=[spec, spec],
        out_specs=pl.BlockSpec((tbs, 3, nj, LANES), lambda r: (r, 0, 0, 0)),
        out_shape=jax.ShapeDtypeStruct((nr * tbs, 3, nj, LANES), jnp.bfloat16),
        compiler_params=params(60 * 1024 * 1024),
    )(velocity, vorticity)


def phase_rows(m_of_slot, points, groups, subs):
    modes = m_of_slot.reshape(-1, groups, subs).transpose(1, 0, 2).reshape(-1)
    paired = jnp.repeat(modes, 2)
    parity = jnp.arange(paired.shape[0], dtype=jnp.int32) % 2
    column = jnp.arange(points, dtype=jnp.int32)
    product = (paired[:, None] * column[None, :] + parity[:, None] * (points // 4)) % points
    angle = 2.0 * math.pi / points * product.astype(jnp.float32)
    return (math.sqrt(2.0 / points) * jnp.cos(angle)).astype(jnp.bfloat16)


def dft_kernel(x_ref, table_ref, out_ref):
    points = table_ref.shape[1]
    grid = jnp.concatenate([x_ref[:, f].reshape(points, LANES) for f in range(3)], axis=1)
    out_ref[...] = jnp.dot(table_ref[...], grid, preferred_element_type=jnp.float32).astype(jnp.bfloat16)


def dft(x, table):
    rows, points = table.shape
    step = 256
    return pl.pallas_call(
        dft_kernel,
        grid=(rows // step,),
        in_specs=[
            pl.BlockSpec(x.shape, lambda i: (0, 0, 0, 0)),
            pl.BlockSpec((step, points), lambda i: (i, 0)),
        ],
        out_specs=pl.BlockSpec((step, 3 * LANES), lambda i: (i, 0)),
        out_shape=jax.ShapeDtypeStruct((rows, 3 * LANES), jnp.bfloat16),
        compiler_params=params(),
    )(x, table)


def matches(source_of, shape):
    row = lax.broadcasted_iota(jnp.int32, shape, 0)
    column = lax.broadcasted_iota(jnp.int32, shape, 1)
    return (source_of(row) == column).astype(jnp.float32).astype(jnp.bfloat16)


def moved_rows(matrix, array):
    return jnp.dot(matrix, array, preferred_element_type=jnp.float32).astype(jnp.bfloat16)


def legendre_kernel(place_ref, y_ref, leg0_ref, leg1_ref, leg2_ref, leg3_ref, out_ref, side):
    place_x, zh = place_ref[0], place_ref[1]
    pair = pl.program_id(0)
    for kk in range(2):
        k = pair * 2 + kk

        def source(i):
            tb, c, z, r = i // 32, (i // 16) % 2, (i // 8) % 2, i % 8
            return ((z * 8 + r) * 4 + tb) * 8 + k * 2 + c

        move = matches(source, (128, 512))
        for h in range(2):
            moved = moved_rows(move, y_ref[h * 512 : (h + 1) * 512, :])
            for tb in range(4):
                for c in range(2):
                    for f in range(3):
                        start = (c * 3 + f) * 32 + h * 16
                        side[kk, start : start + 16, tb * LANES : (tb + 1) * LANES] = moved[
                            (tb * 2 + c) * 16 : (tb * 2 + c) * 16 + 16, f * LANES : (f + 1) * LANES
                        ]
    for e, leg_ref in enumerate((leg0_ref, leg1_ref, leg2_ref, leg3_ref)):
        coeffs = [
            lax.dot_general(
                leg_ref[:, kk].reshape(128, -1),
                side[kk],
                (((1,), (1,)), ((), ())),
                preferred_element_type=jnp.float32,
            ).astype(jnp.bfloat16)
            for kk in range(2)
        ]
        both = jnp.concatenate(coeffs, axis=1)
        for d in range(4):
            out_ref[((place_x - e) & 3) * 4 + ((zh - d) & 3), 0] = both[d * 32 : (d + 1) * 32, :]


def legendre_step(place, y, legs):
    nodes = legs[0].shape[-1]
    return pl.pallas_call(
        legendre_kernel,
        grid=(2,),
        in_specs=[
            pl.BlockSpec(memory_space=pltpu.SMEM),
            pl.BlockSpec(y.shape, lambda p: (0, 0)),
        ]
        + [pl.BlockSpec((4, 2, 32, nodes), lambda p: (0, p, 0, 0))] * 4,
        out_specs=pl.BlockSpec((16, 1, 32, 384), lambda p: (0, p, 0, 0)),
        out_shape=jax.ShapeDtypeStruct((16, 2, 32, 384), jnp.bfloat16),
        scratch_shapes=[pltpu.VMEM((2, 192, nodes), jnp.bfloat16)],
        compiler_params=params(),
    )(place, y, *legs)


def solve_kernel(coeffs_ref, known_ref, inverse_ref, out_ref, side, solved):
    nr = known_ref.shape[-1]
    lanes = matches(lambda i: ((i // 32) % 4) * 128 + (i // 128) * 32 + i % 32, (512, 512))
    swap = matches(lambda i: (i % 16) * 16 + i // 16, (256, 256))
    grouped = []
    for g in range(3):
        wide = jnp.concatenate(
            [coeffs_ref[x, :, :, g * LANES : (g + 1) * LANES].reshape(256, LANES) for x in range(4)], axis=1
        )
        grouped.append(jnp.dot(wide, lanes, preferred_element_type=jnp.float32).astype(jnp.bfloat16))
    for cf in range(6):
        rights = []
        for kk in range(2):
            q = kk * 6 + cf
            coeffs = grouped[q // 4][:, (q % 4) * nr : (q % 4 + 1) * nr].astype(jnp.float32)
            known = known_ref[:, kk, cf].reshape(256, nr).astype(jnp.float32)
            rights.append((known + section_step * coeffs).astype(jnp.bfloat16).reshape(8, 32, nr))
        for h in range(2):
            both = jnp.concatenate([right[:, h * 16 : (h + 1) * 16] for right in rights], axis=0)
            side[h * 16 : (h + 1) * 16, cf * 16 : (cf + 1) * 16] = moved_rows(
                swap, both.reshape(256, nr)
            ).reshape(16, 16, nr)
    for k in range(32):
        solved[k] = lax.dot_general(
            side[k], inverse_ref[k], (((1,), (1,)), ((), ())), preferred_element_type=jnp.float32
        ).astype(jnp.bfloat16)
    for cf in range(6):
        for h in range(2):
            here = solved[h * 16 : (h + 1) * 16, cf * 16 : (cf + 1) * 16]
            back = moved_rows(swap, here.reshape(256, nr)).reshape(2, 8, 16, nr)
            for kk in range(2):
                out_ref[:, kk, cf, h * 16 : (h + 1) * 16] = back[kk]


def radial_solve(coeffs, known, inverse):
    nr = known.shape[-1]
    return pl.pallas_call(
        solve_kernel,
        out_shape=jax.ShapeDtypeStruct(known.shape, jnp.bfloat16),
        scratch_shapes=[pltpu.VMEM((32, 96, nr), jnp.bfloat16)] * 2,
        compiler_params=params(),
    )(coeffs, known, inverse)


def legendre_by_slot(legendre, zh):
    pieces = []
    for d in range(4):
        piece = lax.dynamic_slice_in_dim(legendre, ((zh + d) & 3) * 4, 4, axis=0)
        if d:
            piece = lax.ppermute(piece, "zh", [(i, (i + d) % 4) for i in range(4)])
        pieces.append(piece)
    return pieces


def body(velocity, vorticity, m_of_slot, legendre, known_term, inverse):
    place_x, zh = lax.axis_index("x"), lax.axis_index("zh")
    table = phase_rows(m_of_slot, velocity.shape[2] * 32, 4, 4)
    pieces = legendre_by_slot(legendre, zh)
    table, *pieces = lax.optimization_barrier((table, *pieces))
    blocks = lamb_blocks(velocity, vorticity)
    blocks = lax.all_to_all(blocks, "long", split_axis=0, concat_axis=0, tiled=True)
    blocks, *pieces = lax.optimization_barrier((blocks, *pieces))
    leg = jnp.stack(pieces, axis=0)
    legs = [leg] + [lax.ppermute(leg, "x", [(i, (i + e) % 4) for i in range(4)]) for e in (1, 2, 3)]
    fourier = dft(blocks, table)
    fourier = fourier.reshape(-1, 8, 3 * LANES)
    fourier = lax.all_to_all(fourier, ("zh", "long"), split_axis=0, concat_axis=0, tiled=True)
    coeffs = legendre_step(jnp.stack([place_x, zh]), fourier.reshape(-1, 3 * LANES), legs)
    coeffs = lax.all_to_all(coeffs, ("x", "zh"), split_axis=0, concat_axis=0, tiled=True)
    nr = known_term.shape[-1]
    solved = radial_solve(
        coeffs.reshape(4, 8, 32, 384), known_term.reshape(8, 2, 6, 32, nr), inverse
    )
    return solved.reshape(known_term.shape)


def solution(mesh):
    mesh = Mesh(mesh.devices.reshape(4, 4, 32), ("x", "zh", "long"))
    wide = ("x", "zh")
    return jax.shard_map(
        body,
        mesh=mesh,
        in_specs=(
            P(None, wide, "long", None),
            P(None, wide, "long", None),
            P(),
            P("long", wide, None),
            P("long", None, None, wide, None),
            P(wide, None, None),
        ),
        out_specs=P("long", None, None, wide, None),
        check_vma=False,
    )
```

```python
import math

import jax
import jax.numpy as jnp
from jax import lax
from jax.experimental import pallas as pl
from jax.experimental.pallas import tpu as pltpu
from jax.sharding import Mesh
from jax.sharding import PartitionSpec as P

section_step = 0.75
VMEM_LIMIT = 48 * 1024 * 1024
LARGE = 60 * 1024 * 1024
LANES = 128


def params(limit=VMEM_LIMIT):
    return pltpu.CompilerParams(vmem_limit_bytes=limit)


def lamb_kernel(vel_ref, vort_ref, out_ref):
    tbs = vel_ref.shape[3] // LANES
    for r in range(vel_ref.shape[1]):
        for tb in range(tbs):
            lanes = slice(tb * LANES, (tb + 1) * LANES)
            vel = [vel_ref[i, r, :, lanes].astype(jnp.float32) for i in range(3)]
            vort = [vort_ref[i, r, :, lanes].astype(jnp.float32) for i in range(3)]
            for f in range(3):
                a, b = (f + 1) % 3, (f + 2) % 3
                out_ref[r * tbs + tb, f] = (vel[a] * vort[b] - vel[b] * vort[a]).astype(jnp.bfloat16)


def lamb_blocks(velocity, vorticity):
    _, nr, nj, nt = velocity.shape
    tbs = nt // LANES
    steps = 2
    spec = pl.BlockSpec((3, nr // steps, nj, nt), lambda r: (0, r, 0, 0))
    return pl.pallas_call(
        lamb_kernel,
        grid=(steps,),
        in_specs=[spec, spec],
        out_specs=pl.BlockSpec((nr // steps * tbs, 3, nj, LANES), lambda r: (r, 0, 0, 0)),
        out_shape=jax.ShapeDtypeStruct((nr * tbs, 3, nj, LANES), jnp.bfloat16),
        compiler_params=params(LARGE),
    )(velocity, vorticity)


SINE = (6.283185160089461, -41.341655031412216, 81.6010040730263, -76.54978228858441, 39.53670603021233)


def phase_kernel(mode_ref, out_ref):
    rows, points = out_ref.shape
    column = lax.broadcasted_iota(jnp.int32, (rows, points), 1).astype(jnp.float32)
    parity = (lax.broadcasted_iota(jnp.int32, (rows, 1), 0) & 1).astype(jnp.float32)
    turns = (mode_ref[...] * column + parity * (points / 4)) * (1.0 / points)
    quarter = jnp.abs(turns - jnp.floor(turns) - 0.5) - 0.25
    square = quarter * quarter
    norm = math.sqrt(2.0 / points)
    value = norm * SINE[4]
    for power in (3, 2, 1, 0):
        value = value * square + norm * SINE[power]
    out_ref[...] = (value * quarter).astype(jnp.bfloat16)


def phase_rows(m_of_slot, points, groups, subs):
    modes = m_of_slot.reshape(-1, groups, subs).transpose(1, 0, 2).reshape(-1)
    paired = jnp.repeat(modes, 2).astype(jnp.float32)[:, None]
    rows, step = paired.shape[0], 256
    return pl.pallas_call(
        phase_kernel,
        grid=(rows // step,),
        in_specs=[pl.BlockSpec((step, 1), lambda i: (i, 0))],
        out_specs=pl.BlockSpec((step, points), lambda i: (i, 0)),
        out_shape=jax.ShapeDtypeStruct((rows, points), jnp.bfloat16),
        compiler_params=params(),
    )(paired)


def dft_kernel(x_ref, table_ref, out_ref):
    points = table_ref.shape[1]
    grid = jnp.concatenate([x_ref[:, f].reshape(points, LANES) for f in range(3)], axis=1)
    out_ref[...] = jnp.dot(table_ref[...], grid, preferred_element_type=jnp.float32).astype(jnp.bfloat16)


def dft(x, table):
    rows, points = table.shape
    step = 256
    return pl.pallas_call(
        dft_kernel,
        grid=(rows // step,),
        in_specs=[
            pl.BlockSpec(x.shape, lambda i: (0, 0, 0, 0)),
            pl.BlockSpec((step, points), lambda i: (i, 0)),
        ],
        out_specs=pl.BlockSpec((step, 3 * LANES), lambda i: (i, 0)),
        out_shape=jax.ShapeDtypeStruct((rows, 3 * LANES), jnp.bfloat16),
        compiler_params=params(),
    )(x, table)


def matches(source_of, shape):
    row = lax.broadcasted_iota(jnp.int32, shape, 0)
    column = lax.broadcasted_iota(jnp.int32, shape, 1)
    return (source_of(row) == column).astype(jnp.float32).astype(jnp.bfloat16)


def moved_rows(matrix, array):
    return jnp.dot(matrix, array, preferred_element_type=jnp.float32).astype(jnp.bfloat16)


def legendre_kernel(place_ref, y_ref, leg0_ref, leg1_ref, leg2_ref, leg3_ref, out_ref, side):
    place_x, zh = place_ref[0], place_ref[1]
    pair = pl.program_id(0)
    for kk in range(2):
        k = pair * 2 + kk

        def source(i):
            tb, c, z, r = i // 32, (i // 16) % 2, (i // 8) % 2, i % 8
            return ((z * 8 + r) * 4 + tb) * 8 + k * 2 + c

        move = matches(source, (128, 512))
        for h in range(2):
            moved = moved_rows(move, y_ref[h * 512 : (h + 1) * 512, :])
            for tb in range(4):
                for c in range(2):
                    for f in range(3):
                        start = (c * 3 + f) * 32 + h * 16
                        side[kk, start : start + 16, tb * LANES : (tb + 1) * LANES] = moved[
                            (tb * 2 + c) * 16 : (tb * 2 + c) * 16 + 16, f * LANES : (f + 1) * LANES
                        ]
    for e, leg_ref in enumerate((leg0_ref, leg1_ref, leg2_ref, leg3_ref)):
        coeffs = [
            lax.dot_general(
                leg_ref[:, kk].reshape(128, -1),
                side[kk],
                (((1,), (1,)), ((), ())),
                preferred_element_type=jnp.float32,
            ).astype(jnp.bfloat16)
            for kk in range(2)
        ]
        both = jnp.concatenate(coeffs, axis=1)
        for d in range(4):
            out_ref[((place_x - e) & 3) * 4 + ((zh - d) & 3), 0] = both[d * 32 : (d + 1) * 32, :]


def legendre_step(place, y, legs):
    nodes = legs[0].shape[-1]
    return pl.pallas_call(
        legendre_kernel,
        grid=(2,),
        in_specs=[
            pl.BlockSpec(memory_space=pltpu.SMEM),
            pl.BlockSpec(y.shape, lambda p: (0, 0)),
        ]
        + [pl.BlockSpec((4, 2, 32, nodes), lambda p: (0, p, 0, 0))] * 4,
        out_specs=pl.BlockSpec((16, 1, 32, 384), lambda p: (0, p, 0, 0)),
        out_shape=jax.ShapeDtypeStruct((16, 2, 32, 384), jnp.bfloat16),
        scratch_shapes=[pltpu.VMEM((2, 192, nodes), jnp.bfloat16)],
        compiler_params=params(),
    )(place, y, *legs)


def solve_kernel(coeffs_ref, known_ref, inverse_ref, out_ref, side, solved):
    nr = known_ref.shape[-1]
    lanes = matches(lambda i: ((i // 32) % 4) * 128 + (i // 128) * 32 + i % 32, (512, 512))
    swap = matches(lambda i: (i % 16) * 16 + i // 16, (256, 256))
    grouped = []
    for g in range(3):
        wide = jnp.concatenate(
            [coeffs_ref[x, :, :, g * LANES : (g + 1) * LANES].reshape(256, LANES) for x in range(4)], axis=1
        )
        grouped.append(jnp.dot(wide, lanes, preferred_element_type=jnp.float32).astype(jnp.bfloat16))
    for cf in range(6):
        rights = []
        for kk in range(2):
            q = kk * 6 + cf
            coeffs = grouped[q // 4][:, (q % 4) * nr : (q % 4 + 1) * nr].astype(jnp.float32)
            known = known_ref[:, kk, cf].reshape(256, nr).astype(jnp.float32)
            rights.append((known + section_step * coeffs).astype(jnp.bfloat16).reshape(8, 32, nr))
        for h in range(2):
            both = jnp.concatenate([right[:, h * 16 : (h + 1) * 16] for right in rights], axis=0)
            side[h * 16 : (h + 1) * 16, cf * 16 : (cf + 1) * 16] = moved_rows(
                swap, both.reshape(256, nr)
            ).reshape(16, 16, nr)
    for k in range(32):
        solved[k] = lax.dot_general(
            side[k], inverse_ref[k], (((1,), (1,)), ((), ())), preferred_element_type=jnp.float32
        ).astype(jnp.bfloat16)
    for cf in range(6):
        for h in range(2):
            here = solved[h * 16 : (h + 1) * 16, cf * 16 : (cf + 1) * 16]
            back = moved_rows(swap, here.reshape(256, nr)).reshape(2, 8, 16, nr)
            for kk in range(2):
                out_ref[:, kk, cf, h * 16 : (h + 1) * 16] = back[kk]


def radial_solve(coeffs, known, inverse):
    nr = known.shape[-1]
    return pl.pallas_call(
        solve_kernel,
        out_shape=jax.ShapeDtypeStruct(known.shape, jnp.bfloat16),
        scratch_shapes=[pltpu.VMEM((32, 96, nr), jnp.bfloat16)] * 2,
        compiler_params=params(),
    )(coeffs, known, inverse)


def legendre_by_slot(legendre, zh):
    pieces = []
    for d in range(4):
        piece = lax.dynamic_slice_in_dim(legendre, ((zh + d) & 3) * 4, 4, axis=0)
        if d:
            piece = lax.ppermute(piece, "zh", [(i, (i + d) % 4) for i in range(4)])
        pieces.append(piece)
    return pieces


def body(velocity, vorticity, m_of_slot, legendre, known_term, inverse):
    place_x, zh = lax.axis_index("x"), lax.axis_index("zh")
    table = phase_rows(m_of_slot, velocity.shape[2] * 32, 4, 4)
    pieces = legendre_by_slot(legendre, zh)
    table, *pieces = lax.optimization_barrier((table, *pieces))
    blocks = lamb_blocks(velocity, vorticity)
    blocks = lax.all_to_all(blocks, "long", split_axis=0, concat_axis=0, tiled=True)
    blocks, *pieces = lax.optimization_barrier((blocks, *pieces))
    leg = jnp.stack(pieces, axis=0)
    legs = [leg] + [lax.ppermute(leg, "x", [(i, (i + e) % 4) for i in range(4)]) for e in (1, 2, 3)]
    fourier = dft(blocks, table)
    fourier = fourier.reshape(-1, 8, 3 * LANES)
    fourier = lax.all_to_all(fourier, ("zh", "long"), split_axis=0, concat_axis=0, tiled=True)
    coeffs = legendre_step(jnp.stack([place_x, zh]), fourier.reshape(-1, 3 * LANES), legs)
    coeffs = lax.all_to_all(coeffs, ("x", "zh"), split_axis=0, concat_axis=0, tiled=True)
    nr = known_term.shape[-1]
    solved = radial_solve(
        coeffs.reshape(4, 8, 32, 384), known_term.reshape(8, 2, 6, 32, nr), inverse
    )
    return solved.reshape(known_term.shape)


def solution(mesh):
    mesh = Mesh(mesh.devices.reshape(4, 4, 32), ("x", "zh", "long"))
    wide = ("x", "zh")
    return jax.shard_map(
        body,
        mesh=mesh,
        in_specs=(
            P(None, wide, "long", None),
            P(None, wide, "long", None),
            P(),
            P("long", wide, None),
            P("long", None, None, wide, None),
            P(wide, None, None),
        ),
        out_specs=P("long", None, None, wide, None),
        check_vma=False,
    )
```

```python
import math

import jax
import jax.numpy as jnp
from jax import lax
from jax.experimental import pallas as pl
from jax.experimental.pallas import tpu as pltpu
from jax.sharding import Mesh
from jax.sharding import PartitionSpec as P

section_step = 0.75
VMEM_LIMIT = 48 * 1024 * 1024
LARGE = 60 * 1024 * 1024
LANES = 128


def params(limit=VMEM_LIMIT):
    return pltpu.CompilerParams(vmem_limit_bytes=limit)


def lamb_kernel(vel_ref, vort_ref, out_ref):
    tbs = vel_ref.shape[3] // LANES
    for r in range(vel_ref.shape[1]):
        for tb in range(tbs):
            lanes = slice(tb * LANES, (tb + 1) * LANES)
            vel = [vel_ref[i, r, :, lanes].astype(jnp.float32) for i in range(3)]
            vort = [vort_ref[i, r, :, lanes].astype(jnp.float32) for i in range(3)]
            for f in range(3):
                a, b = (f + 1) % 3, (f + 2) % 3
                out_ref[r * tbs + tb, f] = (vel[a] * vort[b] - vel[b] * vort[a]).astype(jnp.bfloat16)


def lamb_blocks(velocity, vorticity):
    _, nr, nj, nt = velocity.shape
    tbs = nt // LANES
    steps = 2
    spec = pl.BlockSpec((3, nr // steps, nj, nt), lambda r: (0, r, 0, 0))
    return pl.pallas_call(
        lamb_kernel,
        grid=(steps,),
        in_specs=[spec, spec],
        out_specs=pl.BlockSpec((nr // steps * tbs, 3, nj, LANES), lambda r: (r, 0, 0, 0)),
        out_shape=jax.ShapeDtypeStruct((nr * tbs, 3, nj, LANES), jnp.bfloat16),
        compiler_params=params(LARGE),
    )(velocity, vorticity)


SINE = (6.283185160089461, -41.341655031412216, 81.6010040730263, -76.54978228858441, 39.53670603021233)


def phase_kernel(mode_ref, out_ref):
    rows, points = out_ref.shape
    column = lax.broadcasted_iota(jnp.int32, (rows, points), 1).astype(jnp.float32)
    parity = (lax.broadcasted_iota(jnp.int32, (rows, 1), 0) & 1).astype(jnp.float32)
    turns = (mode_ref[...] * column + parity * (points / 4)) * (1.0 / points)
    quarter = jnp.abs(turns - jnp.floor(turns) - 0.5) - 0.25
    square = quarter * quarter
    norm = math.sqrt(2.0 / points)
    value = norm * SINE[4]
    for power in (3, 2, 1, 0):
        value = value * square + norm * SINE[power]
    out_ref[...] = (value * quarter).astype(jnp.bfloat16)


def phase_rows(m_of_slot, points):
    paired = jnp.repeat(m_of_slot, 2).astype(jnp.float32)[:, None]
    rows, step = paired.shape[0], 256
    return pl.pallas_call(
        phase_kernel,
        grid=(rows // step,),
        in_specs=[pl.BlockSpec((step, 1), lambda i: (i, 0))],
        out_specs=pl.BlockSpec((step, points), lambda i: (i, 0)),
        out_shape=jax.ShapeDtypeStruct((rows, points), jnp.bfloat16),
        compiler_params=params(),
    )(paired)


def dft_kernel(x_ref, table_ref, out_ref):
    points = table_ref.shape[1]
    grid = jnp.concatenate([x_ref[:, f].reshape(points, LANES) for f in range(3)], axis=1)
    out_ref[...] = jnp.dot(table_ref[...], grid, preferred_element_type=jnp.float32).astype(jnp.bfloat16)


def dft(x, table):
    rows, points = table.shape
    step = 256
    return pl.pallas_call(
        dft_kernel,
        grid=(rows // step,),
        in_specs=[
            pl.BlockSpec(x.shape, lambda i: (0, 0, 0, 0)),
            pl.BlockSpec((step, points), lambda i: (i, 0)),
        ],
        out_specs=pl.BlockSpec((step, 3 * LANES), lambda i: (i, 0)),
        out_shape=jax.ShapeDtypeStruct((rows, 3 * LANES), jnp.bfloat16),
        compiler_params=params(),
    )(x, table)


def matches(source_of, shape):
    row = lax.broadcasted_iota(jnp.int32, shape, 0)
    column = lax.broadcasted_iota(jnp.int32, shape, 1)
    return (source_of(row) == column).astype(jnp.float32).astype(jnp.bfloat16)


def moved_rows(matrix, array):
    return jnp.dot(matrix, array, preferred_element_type=jnp.float32).astype(jnp.bfloat16)


def legendre_kernel(place_ref, y_ref, leg0_ref, leg1_ref, leg2_ref, leg3_ref, out_ref, side):
    place_x, zh = place_ref[0], place_ref[1]
    pair = pl.program_id(0)
    for kk in range(2):
        k = pair * 2 + kk

        def source(i):
            tb, c, z, r = i // 32, (i // 16) % 2, (i // 4) % 4, i % 4
            return ((r * 4 + tb) * 4 + z) * 8 + k * 2 + c

        move = matches(source, (128, 512))
        for h in range(2):
            moved = moved_rows(move, y_ref[h * 512 : (h + 1) * 512, :])
            for tb in range(4):
                for c in range(2):
                    for f in range(3):
                        start = (c * 3 + f) * 32 + h * 16
                        side[kk, start : start + 16, tb * LANES : (tb + 1) * LANES] = moved[
                            (tb * 2 + c) * 16 : (tb * 2 + c) * 16 + 16, f * LANES : (f + 1) * LANES
                        ]
    for e, leg_ref in enumerate((leg0_ref, leg1_ref, leg2_ref, leg3_ref)):
        coeffs = [
            lax.dot_general(
                leg_ref[:, kk].reshape(128, -1),
                side[kk],
                (((1,), (1,)), ((), ())),
                preferred_element_type=jnp.float32,
            ).astype(jnp.bfloat16)
            for kk in range(2)
        ]
        both = jnp.concatenate(coeffs, axis=1)
        for d in range(4):
            out_ref[((zh - d) & 3) * 4 + ((place_x - e - place_ref[2 + d]) & 3), 0] = both[d * 32 : (d + 1) * 32, :]


def legendre_step(place, y, legs):
    nodes = legs[0].shape[-1]
    return pl.pallas_call(
        legendre_kernel,
        grid=(2,),
        in_specs=[
            pl.BlockSpec(memory_space=pltpu.SMEM),
            pl.BlockSpec(y.shape, lambda p: (0, 0)),
        ]
        + [pl.BlockSpec((4, 2, 32, nodes), lambda p: (0, p, 0, 0))] * 4,
        out_specs=pl.BlockSpec((16, 1, 32, 384), lambda p: (0, p, 0, 0)),
        out_shape=jax.ShapeDtypeStruct((16, 2, 32, 384), jnp.bfloat16),
        scratch_shapes=[pltpu.VMEM((2, 192, nodes), jnp.bfloat16)],
        compiler_params=params(),
    )(place, y, *legs)


def solve_kernel(coeffs_ref, known_ref, inverse_ref, out_ref, side, solved):
    nr = known_ref.shape[-1]
    lanes = matches(
        lambda i: ((i // 32) % 4) * 128 + (i // 128) * 32 + ((i // 4) % 4) * 8 + ((i // 16) % 2) * 4 + i % 4,
        (512, 512),
    )
    swap = matches(lambda i: (i % 16) * 16 + i // 16, (256, 256))
    grouped = []
    for g in range(3):
        wide = jnp.concatenate(
            [coeffs_ref[:, x, :, :, g * LANES : (g + 1) * LANES].reshape(256, LANES) for x in range(4)], axis=1
        )
        grouped.append(jnp.dot(wide, lanes, preferred_element_type=jnp.float32).astype(jnp.bfloat16))
    for cf in range(6):
        rights = []
        for kk in range(2):
            q = kk * 6 + cf
            coeffs = grouped[q // 4][:, (q % 4) * nr : (q % 4 + 1) * nr].astype(jnp.float32)
            known = known_ref[:, kk, cf].reshape(256, nr).astype(jnp.float32)
            rights.append((known + section_step * coeffs).astype(jnp.bfloat16).reshape(8, 32, nr))
        for h in range(2):
            both = jnp.concatenate([right[:, h * 16 : (h + 1) * 16] for right in rights], axis=0)
            side[h * 16 : (h + 1) * 16, cf * 16 : (cf + 1) * 16] = moved_rows(
                swap, both.reshape(256, nr)
            ).reshape(16, 16, nr)
    for k in range(32):
        solved[k] = lax.dot_general(
            side[k], inverse_ref[k], (((1,), (1,)), ((), ())), preferred_element_type=jnp.float32
        ).astype(jnp.bfloat16)
    for cf in range(6):
        for h in range(2):
            here = solved[h * 16 : (h + 1) * 16, cf * 16 : (cf + 1) * 16]
            back = moved_rows(swap, here.reshape(256, nr)).reshape(2, 8, 16, nr)
            for kk in range(2):
                out_ref[:, kk, cf, h * 16 : (h + 1) * 16] = back[kk]


def radial_solve(coeffs, known, inverse):
    nr = known.shape[-1]
    return pl.pallas_call(
        solve_kernel,
        out_shape=jax.ShapeDtypeStruct(known.shape, jnp.bfloat16),
        scratch_shapes=[pltpu.VMEM((32, 96, nr), jnp.bfloat16)] * 2,
        compiler_params=params(),
    )(coeffs, known, inverse)


def live(x, zh, long):
    last_degree = (x * 4 + zh) * 32 + 31
    return last_degree >= long * 16 - 31


def aside(zl):
    return ((0, 0, 0, 0), (0, 0, 0, 0), (0, 0, 2, 0), (0, 1, 1, 1))[zl]


def send_live(array, axis, shift):
    pairs = []
    for x in range(4):
        for zh in range(4):
            for long in range(32):
                off = aside(long // 8)
                if axis == "x":
                    to = ((x + shift) % 4 * 4 + zh) * 32 + long
                    sent = any(live((x - off[d]) % 4, (zh - d) % 4, long) for d in range(4))
                else:
                    to = ((x + off[shift]) % 4 * 4 + (zh + shift) % 4) * 32 + long
                    sent = live(x, zh, long)
                if sent:
                    pairs.append(((x * 4 + zh) * 32 + long, to))
    return lax.ppermute(array, ("x", "zh", "long"), pairs)


def legendre_by_slot(legendre, zh):
    pieces = []
    for d in range(4):
        piece = lax.dynamic_slice_in_dim(legendre, ((zh + d) & 3) * 4, 4, axis=0)
        if d:
            piece = send_live(piece, "zh", d)
        pieces.append(piece)
    return pieces


def body(velocity, vorticity, m_of_slot, legendre, known_term, inverse):
    place_x, zh = lax.axis_index("x"), lax.axis_index("zh")
    table = phase_rows(m_of_slot, velocity.shape[2] * 32)
    pieces = legendre_by_slot(legendre, zh)
    aside_here = jnp.array([aside(zl) for zl in range(4)], jnp.int32)[lax.axis_index("long") // 8]
    place = jnp.concatenate([jnp.stack([place_x, zh]), aside_here])
    table, *pieces = lax.optimization_barrier((table, *pieces))
    blocks = lamb_blocks(velocity, vorticity)
    blocks = lax.all_to_all(blocks, "long", split_axis=0, concat_axis=0, tiled=True)
    blocks, *pieces = lax.optimization_barrier((blocks, *pieces))
    leg = jnp.stack(pieces, axis=0)
    legs = [leg] + [send_live(leg, "x", e) for e in (1, 2, 3)]
    fourier = dft(blocks, table)
    fourier = fourier.reshape(-1, 8, 3 * LANES)
    fourier = lax.all_to_all(fourier, ("long", "zh"), split_axis=0, concat_axis=0, tiled=True)
    coeffs = legendre_step(place, fourier.reshape(-1, 3 * LANES), legs)
    coeffs = lax.all_to_all(coeffs, ("zh", "x"), split_axis=0, concat_axis=0, tiled=True)
    nr = known_term.shape[-1]
    solved = radial_solve(
        coeffs.reshape(4, 4, 2, 32, 384), known_term.reshape(8, 2, 6, 32, nr), inverse
    )
    return solved.reshape(known_term.shape)


def solution(mesh):
    mesh = Mesh(mesh.devices.reshape(4, 4, 32), ("x", "zh", "long"))
    wide = ("x", "zh")
    return jax.shard_map(
        body,
        mesh=mesh,
        in_specs=(
            P(None, wide, "long", None),
            P(None, wide, "long", None),
            P(),
            P("long", wide, None),
            P("long", None, None, wide, None),
            P(wide, None, None),
        ),
        out_specs=P("long", None, None, wide, None),
        check_vma=False,
    )
```

```python
import math

import jax
import jax.numpy as jnp
from jax import lax
from jax.experimental import pallas as pl
from jax.experimental.pallas import tpu as pltpu
from jax.sharding import Mesh
from jax.sharding import PartitionSpec as P

section_step = 0.75
VMEM_LIMIT = 48 * 1024 * 1024
LARGE = 60 * 1024 * 1024
LANES = 128


def params(limit=VMEM_LIMIT):
    return pltpu.CompilerParams(vmem_limit_bytes=limit)


def lamb_kernel(vel_ref, vort_ref, out_ref):
    tbs = vel_ref.shape[3] // LANES
    for r in range(vel_ref.shape[1]):
        for tb in range(tbs):
            lanes = slice(tb * LANES, (tb + 1) * LANES)
            vel = [vel_ref[i, r, :, lanes].astype(jnp.float32) for i in range(3)]
            vort = [vort_ref[i, r, :, lanes].astype(jnp.float32) for i in range(3)]
            for f in range(3):
                a, b = (f + 1) % 3, (f + 2) % 3
                out_ref[r * tbs + tb, f] = (vel[a] * vort[b] - vel[b] * vort[a]).astype(jnp.bfloat16)


def lamb_blocks(velocity, vorticity):
    _, nr, nj, nt = velocity.shape
    tbs = nt // LANES
    steps = 2
    spec = pl.BlockSpec((3, nr // steps, nj, nt), lambda r: (0, r, 0, 0))
    return pl.pallas_call(
        lamb_kernel,
        grid=(steps,),
        in_specs=[spec, spec],
        out_specs=pl.BlockSpec((nr // steps * tbs, 3, nj, LANES), lambda r: (r, 0, 0, 0)),
        out_shape=jax.ShapeDtypeStruct((nr * tbs, 3, nj, LANES), jnp.bfloat16),
        compiler_params=params(LARGE),
    )(velocity, vorticity)


SINE = (6.283185160089461, -41.341655031412216, 81.6010040730263, -76.54978228858441, 39.53670603021233)


def phase_kernel(mode_ref, out_ref):
    rows, points = out_ref.shape
    column = lax.broadcasted_iota(jnp.int32, (rows, points), 1).astype(jnp.float32)
    parity = (lax.broadcasted_iota(jnp.int32, (rows, 1), 0) & 1).astype(jnp.float32)
    turns = (mode_ref[...] * column + parity * (points / 4)) * (1.0 / points)
    quarter = jnp.abs(turns - jnp.floor(turns) - 0.5) - 0.25
    square = quarter * quarter
    norm = math.sqrt(2.0 / points)
    value = norm * SINE[4]
    for power in (3, 2, 1, 0):
        value = value * square + norm * SINE[power]
    out_ref[...] = (value * quarter).astype(jnp.bfloat16)


def phase_rows(m_of_slot, points):
    paired = jnp.repeat(m_of_slot, 2).astype(jnp.float32)[:, None]
    rows, step = paired.shape[0], 256
    return pl.pallas_call(
        phase_kernel,
        grid=(rows // step,),
        in_specs=[pl.BlockSpec((step, 1), lambda i: (i, 0))],
        out_specs=pl.BlockSpec((step, points), lambda i: (i, 0)),
        out_shape=jax.ShapeDtypeStruct((rows, points), jnp.bfloat16),
        compiler_params=params(),
    )(paired)


def dft_kernel(x_ref, table_ref, out_ref):
    points = table_ref.shape[1]
    grid = jnp.concatenate([x_ref[:, f].reshape(points, LANES) for f in range(3)], axis=1)
    step = 256

    @pl.loop(0, table_ref.shape[0] // step)
    def _(i):
        rows = pl.ds(pl.multiple_of(i * step, step), step)
        out_ref[rows, :] = jnp.dot(
            table_ref[rows, :], grid, preferred_element_type=jnp.float32
        ).astype(jnp.bfloat16)


def dft(x, table):
    rows = table.shape[0]
    return pl.pallas_call(
        dft_kernel,
        in_specs=[pl.BlockSpec(memory_space=pltpu.VMEM)] * 2,
        out_specs=pl.BlockSpec(memory_space=pltpu.VMEM),
        out_shape=jax.ShapeDtypeStruct((rows, 3 * LANES), jnp.bfloat16),
        compiler_params=params(),
    )(x, table)


def matches(source_of, shape):
    row = lax.broadcasted_iota(jnp.int32, (shape[0], 1), 0)
    column = lax.broadcasted_iota(jnp.int32, shape, 1)
    return (source_of(row) == column).astype(jnp.float32).astype(jnp.bfloat16)


def moved_rows(matrix, array):
    return jnp.dot(matrix, array, preferred_element_type=jnp.float32).astype(jnp.bfloat16)


def legendre_kernel(place_ref, y_ref, leg0_ref, leg1_ref, leg2_ref, leg3_ref, out_ref, side):
    place_x, zh = place_ref[0], place_ref[1]
    for kk in range(4):
        k, pair, odd = kk, kk // 2, kk % 2

        def source(i):
            tb, c, z, r = i >> 5, (i >> 4) & 1, (i >> 2) & 3, i & 3
            return ((r * 4 + tb) * 4 + z) * 8 + k * 2 + c

        move = matches(source, (128, 512))
        for h in range(2):
            moved = moved_rows(move, y_ref[h * 512 : (h + 1) * 512, :])
            for tb in range(4):
                for c in range(2):
                    for f in range(3):
                        start = (c * 3 + f) * 32 + h * 16
                        side[odd, start : start + 16, tb * LANES : (tb + 1) * LANES] = moved[
                            (tb * 2 + c) * 16 : (tb * 2 + c) * 16 + 16, f * LANES : (f + 1) * LANES
                        ]
        if odd:
            for e, leg_ref in enumerate((leg0_ref, leg1_ref, leg2_ref, leg3_ref)):
                coeffs = [
                    lax.dot_general(
                        leg_ref[:, pair * 2 + i].reshape(128, -1),
                        side[i],
                        (((1,), (1,)), ((), ())),
                        preferred_element_type=jnp.float32,
                    ).astype(jnp.bfloat16)
                    for i in range(2)
                ]
                both = jnp.concatenate(coeffs, axis=1)
                for d in range(4):
                    to = ((zh - d) & 3) * 4 + ((place_x - e - place_ref[2 + d]) & 3)
                    out_ref[to, pair] = both[d * 32 : (d + 1) * 32, :]


def legendre_step(place, y, legs):
    nodes = legs[0].shape[-1]
    return pl.pallas_call(
        legendre_kernel,
        in_specs=[pl.BlockSpec(memory_space=pltpu.SMEM)] + [pl.BlockSpec(memory_space=pltpu.VMEM)] * 5,
        out_specs=pl.BlockSpec(memory_space=pltpu.VMEM),
        out_shape=jax.ShapeDtypeStruct((16, 2, 32, 384), jnp.bfloat16),
        scratch_shapes=[pltpu.VMEM((2, 192, nodes), jnp.bfloat16)],
        compiler_params=params(),
    )(place, y, *legs)


def solve_kernel(coeffs_ref, known_ref, inverse_ref, out_ref, side, solved):
    nr = known_ref.shape[-1]
    lanes = matches(
        lambda i: ((i >> 5) & 3) * 128 + (i >> 7) * 32 + ((i >> 2) & 3) * 8 + ((i >> 4) & 1) * 4 + (i & 3),
        (512, 512),
    )
    swap = matches(lambda i: (i & 15) * 16 + (i >> 4), (256, 256))
    grouped = []
    for g in range(3):
        wide = jnp.concatenate(
            [coeffs_ref[:, x, :, :, g * LANES : (g + 1) * LANES].reshape(256, LANES) for x in range(4)], axis=1
        )
        grouped.append(jnp.dot(wide, lanes, preferred_element_type=jnp.float32).astype(jnp.bfloat16))
    for cf in range(6):
        rights = []
        for kk in range(2):
            q = kk * 6 + cf
            coeffs = grouped[q // 4][:, (q % 4) * nr : (q % 4 + 1) * nr].astype(jnp.float32)
            known = known_ref[:, kk, cf].reshape(256, nr).astype(jnp.float32)
            rights.append((known + section_step * coeffs).astype(jnp.bfloat16).reshape(8, 32, nr))
        for h in range(2):
            both = jnp.concatenate([right[:, h * 16 : (h + 1) * 16] for right in rights], axis=0)
            side[h * 16 : (h + 1) * 16, cf * 16 : (cf + 1) * 16] = moved_rows(
                swap, both.reshape(256, nr)
            ).reshape(16, 16, nr)
    for k in range(32):
        solved[k] = lax.dot_general(
            side[k], inverse_ref[k], (((1,), (1,)), ((), ())), preferred_element_type=jnp.float32
        ).astype(jnp.bfloat16)
    for cf in range(6):
        for h in range(2):
            here = solved[h * 16 : (h + 1) * 16, cf * 16 : (cf + 1) * 16]
            back = moved_rows(swap, here.reshape(256, nr)).reshape(2, 8, 16, nr)
            for kk in range(2):
                out_ref[:, kk, cf, h * 16 : (h + 1) * 16] = back[kk]


def radial_solve(coeffs, known, inverse):
    nr = known.shape[-1]
    return pl.pallas_call(
        solve_kernel,
        out_shape=jax.ShapeDtypeStruct(known.shape, jnp.bfloat16),
        scratch_shapes=[pltpu.VMEM((32, 96, nr), jnp.bfloat16)] * 2,
        compiler_params=params(),
    )(coeffs, known, inverse)


def live(x, zh, long):
    last_degree = (x * 4 + zh) * 32 + 31
    return last_degree >= long * 16 - 31


def aside(zl):
    return ((0, 0, 0, 0), (0, 0, 0, 0), (0, 0, 2, 0), (0, 1, 1, 1))[zl]


def send_live(array, axis, shift):
    pairs = []
    for x in range(4):
        for zh in range(4):
            for long in range(32):
                off = aside(long // 8)
                if axis == "x":
                    to = ((x + shift) % 4 * 4 + zh) * 32 + long
                    sent = any(live((x - off[d]) % 4, (zh - d) % 4, long) for d in range(4))
                else:
                    to = ((x + off[shift]) % 4 * 4 + (zh + shift) % 4) * 32 + long
                    sent = live(x, zh, long)
                if sent:
                    pairs.append(((x * 4 + zh) * 32 + long, to))
    return lax.ppermute(array, ("x", "zh", "long"), pairs)


def legendre_by_slot(legendre, zh):
    pieces = []
    for d in (0, 1, 3, 2):
        piece = lax.dynamic_slice_in_dim(legendre, ((zh + d) & 3) * 4, 4, axis=0)
        if d:
            piece = send_live(piece, "zh", d)
        pieces.append(piece)
    return pieces


def body(velocity, vorticity, m_of_slot, legendre, known_term, inverse):
    place_x, zh = lax.axis_index("x"), lax.axis_index("zh")
    table = phase_rows(m_of_slot, velocity.shape[2] * 32)
    pieces = legendre_by_slot(legendre, zh)
    aside_here = jnp.array([aside(zl) for zl in range(4)], jnp.int32)[lax.axis_index("long") // 8]
    place = jnp.concatenate([jnp.stack([place_x, zh]), aside_here])
    table, *pieces = lax.optimization_barrier((table, *pieces))
    blocks = lamb_blocks(velocity, vorticity)
    blocks = lax.all_to_all(blocks, "long", split_axis=0, concat_axis=0, tiled=True)
    blocks, *pieces = lax.optimization_barrier((blocks, *pieces))
    leg = jnp.stack([pieces[0], pieces[1], pieces[3], pieces[2]], axis=0)
    legs = [leg] + [send_live(leg, "x", e) for e in (1, 2, 3)]
    fourier = dft(blocks, table)
    fourier = fourier.reshape(-1, 8, 3 * LANES)
    fourier = lax.all_to_all(fourier, ("long", "zh"), split_axis=0, concat_axis=0, tiled=True)
    coeffs = legendre_step(place, fourier.reshape(-1, 3 * LANES), legs)
    coeffs = lax.all_to_all(coeffs, ("zh", "x"), split_axis=0, concat_axis=0, tiled=True)
    nr = known_term.shape[-1]
    solved = radial_solve(
        coeffs.reshape(4, 4, 2, 32, 384), known_term.reshape(8, 2, 6, 32, nr), inverse
    )
    return solved.reshape(known_term.shape)


def solution(mesh):
    mesh = Mesh(mesh.devices.reshape(4, 4, 32), ("x", "zh", "long"))
    wide = ("x", "zh")
    return jax.shard_map(
        body,
        mesh=mesh,
        in_specs=(
            P(None, wide, "long", None),
            P(None, wide, "long", None),
            P(),
            P("long", wide, None),
            P("long", None, None, wide, None),
            P(wide, None, None),
        ),
        out_specs=P("long", None, None, wide, None),
        check_vma=False,
    )
```
